256 devices in a mesh: wide: 32 (over y_lo, z, core), narrow: 8 (over y_hi, x).
Axes of the slice: x: 4, y: 4 (y_hi: 2, y_lo: 2; y = y_hi * 2 + y_lo), z: 8, core: 2. Of those that a mesh axis runs over, the one named last changes fastest.
Arguments:
- mentions: bfloat16 [16384, 768], P('wide'), may hold values from -16 to 16
- gold_vectors: bfloat16 [16384, 768], P('wide'), may hold values from -2 to 2
- gold_ids: int32 [16384], P('wide'), may hold values from 0 to 511
- cache: bfloat16 [32768, 768], P(('wide', 'narrow')), may hold values from -4 to 4
- cache_ids: int32 [32768], P(('wide', 'narrow')), may hold values from 0 to 511
Outputs:
- loss: float32 [16384], P('wide')
- mention_grad: float32 [16384, 768], P(('wide', 'narrow'))
The draws below stay inside these ranges and needn't reach their ends.
All inputs are finite; a program needn't handle non-finite values.
Results may differ from the reference program's by a relative error of at most 0.0015.
Values may be sent and summed in bfloat16 or wider, within the bound.
A program may use at most 64 MiB of HBM per device.

```python
import math
import jax
import jax.numpy as jnp
from jax import lax

D = 768
ROWS_DEV = 128
MENTIONS = 16384
CACHE = 32768
ENTITIES = 512
N_NARROW = 8


def world(key):
    gold = jax.random.randint(jax.random.fold_in(key, 101), (MENTIONS,), 0, ENTITIES)
    owners = jax.random.randint(jax.random.fold_in(key, 102), (CACHE,), 0, ENTITIES)
    table = jnp.clip(jax.random.normal(jax.random.fold_in(key, 103), (ENTITIES, D), jnp.float32), -5.0, 5.0) * D ** (-0.25)
    return (gold, owners, table)


def cache_rows(key, owners, table):
    noise = jnp.clip(jax.random.normal(jax.random.fold_in(key, 104), (CACHE, D), jnp.float32), -5.0, 5.0) * D ** (-0.25)
    spread = jnp.exp(jax.random.uniform(jax.random.fold_in(key, 105), (CACHE,), jnp.float32, math.log(0.5), math.log(2.0)))
    position = jnp.arange(CACHE)
    rising = 0.7 + 0.8 * (position // ROWS_DEV % N_NARROW).astype(jnp.float32) / max(N_NARROW - 1, 1)
    scale = jnp.where(position % 64 == 2, 1.0, spread * rising)
    rows = 0.47 * table[owners] + 0.88 * scale[:, None] * noise
    partner = jnp.clip(jax.random.normal(jax.random.fold_in(key, 106), (CACHE // 64, D), jnp.float32), -5.0, 5.0) * D ** (-0.25)
    grouped = rows.reshape(CACHE // 64, 64, D)
    grouped = grouped.at[:, 3, :].set(grouped[:, 2, :] + 0.25 * partner)
    return grouped.reshape(CACHE, D)


def draw_mentions(key, part):
    gold, owners, table = world(key)
    key = jax.random.fold_in(key, 1)
    noise = jnp.clip(jax.random.normal(key, (MENTIONS, D), jnp.float32), -5.0, 5.0) * D ** (-0.25)
    values = 0.47 * table[gold] + 0.88 * noise
    return values.astype(jnp.bfloat16)


def draw_gold_vectors(key, part):
    gold, owners, table = world(key)
    key = jax.random.fold_in(key, 2)
    noise = jnp.clip(jax.random.normal(key, (MENTIONS, D), jnp.float32), -5.0, 5.0) * D ** (-0.25)
    return (0.47 * table[gold] + 0.88 * noise).astype(jnp.bfloat16)


def draw_cache(key, part):
    gold, owners, table = world(key)
    return cache_rows(key, owners, table).astype(jnp.bfloat16)


def draw_gold_ids(key, part):
    gold, owners, table = world(key)
    return gold.astype(jnp.int32)


def draw_cache_ids(key, part):
    gold, owners, table = world(key)
    return owners.astype(jnp.int32)


def setup_inputs(seed: int = 0) -> dict:
    seeds = jax.random.split(jax.random.key(seed), 6)
    return {
        "mentions": draw_mentions(jax.random.fold_in(seeds[5], 71), 0),
        "gold_vectors": draw_gold_vectors(jax.random.fold_in(seeds[5], 71), 0),
        "gold_ids": draw_gold_ids(jax.random.fold_in(seeds[5], 71), 0),
        "cache": draw_cache(jax.random.fold_in(seeds[5], 71), 0),
        "cache_ids": draw_cache_ids(jax.random.fold_in(seeds[5], 71), 0),
    }


NEG = -1e30


def reference(mentions, gold_vectors, gold_ids, cache, cache_ids):
    gold_score = jnp.sum(mentions.astype(jnp.float32) * gold_vectors.astype(jnp.float32), axis=1)
    width = math.gcd(CACHE, 2048)
    blocks = CACHE // width
    cache_blocks = cache.reshape(blocks, width, D)
    id_blocks = cache_ids.reshape(blocks, width)

    def scores_of(block, ids):
        scores = lax.dot_general(block, mentions, (((1,), (1,)), ((), ())), preferred_element_type=jnp.float32)
        allowed = ids[:, None] != gold_ids[None, :]
        return scores, allowed

    def forward(carry, item):
        running, total = carry
        scores, allowed = scores_of(item[0], item[1])
        block_top = jnp.max(jnp.where(allowed, scores, NEG), axis=0)
        newest = jnp.maximum(running, block_top)
        total = total * jnp.exp(running - newest) + jnp.sum(jnp.exp(jnp.where(allowed, scores - newest[None, :], NEG)), axis=0)
        return (newest, total), None

    start = (jnp.full((MENTIONS,), NEG, jnp.float32), jnp.zeros((MENTIONS,), jnp.float32))
    (running, total), unused = lax.scan(forward, start, (cache_blocks, id_blocks))
    highest = jnp.maximum(running, gold_score)
    whole = total * jnp.exp(running - highest) + jnp.exp(gold_score - highest)
    lse = highest + jnp.log(whole)
    loss = lse - gold_score

    def backward(grad, item):
        scores, allowed = scores_of(item[0], item[1])
        weights = jnp.exp(jnp.where(allowed, scores - lse[None, :], NEG)).astype(jnp.bfloat16)
        grad = grad + lax.dot_general(weights, item[0], (((0,), (0,)), ((), ())), preferred_element_type=jnp.float32)
        return grad, None

    grad, unused = lax.scan(backward, jnp.zeros((MENTIONS, D), jnp.float32), (cache_blocks, id_blocks))
    mention_grad = grad + (jnp.exp(gold_score - lse) - 1.0)[:, None] * gold_vectors.astype(jnp.float32)
    return loss, mention_grad
```

```python
import functools

import jax
import jax.numpy as jnp
from jax import lax
from jax.experimental import pallas as pl
from jax.experimental.pallas import tpu as pltpu
from jax.sharding import PartitionSpec as P

MESH = pl.DeviceIdType.MESH
NEG = -1e30
FLOOR = -1e20
NX, NY, NZ = 4, 4, 8
PIECES = 2
LEVELS = 32766.0
TINY = 1e-35
PEERS = ((2, 1), (1, 1), (3, 1), (2, 0), (0, 1), (1, 0), (3, 0))
ORDER = (0, 8, 1, 2, 9, 10, 3, 4, 11, 12, 5, 6, 13, 14, 7, 15)
EVENTS = (
    (),
    (("y", 0),),
    (("z", 1), ("z", 2)),
    (),
    (("y", 1),),
    (("y", 2),),
    (("z", 3), ("z", 4)),
    (),
    (("y", 3),),
    (("y", 4),),
    (("z", 5), ("z", 6)),
    (),
    (("y", 5),),
    (("z", 7), ("y", 6)),
    (),
    (("y", 7),),
)


def place(x, y, z, c):
    return ((y % 2 * NZ + z) * 2 + c, (y // 2) * NX + x)


def kernel(
    mentions_hbm, gold_hbm, gold_ids_ref, cache_hbm, cache_ids_ref, loss_ref, grad_ref,
    buf, ids, men, gold, gid, gscore, run, low, u, q, rq, stat, rstat, fac, turned,
    local_sem, zs, zr, ys, yr, cs, cr, qs, qr, ss, sr,
):
    w = lax.axis_index("wide")
    n = lax.axis_index("narrow")
    c = w % 2
    z = (w // 2) % NZ
    y = (n // NX) * 2 + w // (2 * NZ)
    x = n % NX
    rows = buf.shape[2]
    piece = rows // PIECES
    part = grad_ref.shape[0]

    up = place(x, y, (z + 1) % NZ, c)
    down = place(x, y, (z + NZ - 1) % NZ, c)
    side = place(x, (y + NY + 1 - 2 * c) % NY, z, c)
    other_side = place(x, (y + NY - 1 + 2 * c) % NY, z, c)
    twin = place(x, y, z, 1 - c)

    def peer(dx, dy, sign):
        return place((x + NX + sign * dx) % NX, (y + 2 * dy) % NY, z, c)

    load_c = pltpu.make_async_copy(cache_hbm, buf.at[0, c], local_sem.at[0])
    load_m = pltpu.make_async_copy(mentions_hbm, men, local_sem.at[1])
    load_g = pltpu.make_async_copy(gold_hbm, gold, local_sem.at[2])
    load_c.start()
    load_m.start()
    load_g.start()
    ids[0, c] = cache_ids_ref[...]

    barrier = pltpu.get_barrier_semaphore()
    sources = [up, down, other_side, twin] + [peer(dx, dy, -1) for dx, dy in PEERS]
    for d in sources:
        pl.semaphore_signal(barrier, inc=1, device_id=d, device_id_type=MESH)

    def moved(src, dst, send, recv, index, core, target, p):
        if p == PIECES:
            source, goal = ids.at[src, core], ids.at[dst, core]
        else:
            s = pl.ds(p * piece, piece)
            source, goal = buf.at[src, core, s], buf.at[dst, core, s]
        return pltpu.make_async_remote_copy(
            src_ref=source, dst_ref=goal, send_sem=send.at[index, p], recv_sem=recv.at[index, p],
            device_id=target, device_id_type=MESH)

    def z_copy(src, dst, target, p):
        return moved(src, dst, zs, zr, dst, c, target, p)

    def y_copy(src, p):
        return moved(src, 8 + src, ys, yr, src, c, side, p)

    def twin_copy(src, p):
        return moved(src, src, cs, cr, src, c, twin, p)

    def twin_arrival(src, p):
        return moved(src, src, cs, cr, src, 1 - c, twin, p)

    def onward(k, p):
        if k == 0:
            z_copy(0, 1, up, p).start()
            z_copy(0, 2, down, p).start()
        elif k in (1, 3):
            z_copy(k, k + 2, up, p).start()
        elif k in (2, 4):
            z_copy(k, k + 2, down, p).start()
        elif k == 5:
            pl.when(c == 0)(lambda: z_copy(5, 7, up, p).start())
        elif k == 6:
            pl.when(c == 1)(lambda: z_copy(6, 7, down, p).start())
        y_copy(k, p).start()
        twin_copy(k, p).start()

    def z_arrived(k, p):
        z_copy(k, k, up, p).wait_recv()

    def y_arrived(k, p):
        y_copy(k, p).wait_recv()

    def handle(events):
        for p in (PIECES,) + tuple(range(PIECES)):
            for kind, k in events:
                if kind == "z":
                    z_arrived(k, p)
                    onward(k, p)
                else:
                    y_arrived(k, p)
                    twin_copy(8 + k, p).start()

    pl.semaphore_wait(barrier, len(sources))
    load_c.wait()
    for p in (PIECES,) + tuple(range(PIECES)):
        onward(0, p)

    run[...] = jnp.full(run.shape, FLOOR, jnp.float32)
    low[...] = jnp.zeros(low.shape, jnp.float32)
    u[...] = jnp.zeros(u.shape, jnp.float32)
    fac[...] = jnp.zeros(fac.shape, jnp.float32)
    blocks = men.shape[0] // 128
    for b in range(blocks):
        row = jnp.broadcast_to(gold_ids_ref[pl.ds(b, 1), :].astype(jnp.float32), (128, 128))
        gid[pl.ds(b * 128, 128), :] = row.T
    load_m.wait()
    load_g.wait()

    def gold_block(b, _):
        s = pl.ds(pl.multiple_of(b * 128, 128), 128)
        both = men[s, :].astype(jnp.float32) * gold[s, :].astype(jnp.float32)
        score = jnp.broadcast_to(jnp.sum(both, axis=1, keepdims=True), (128, 128))
        gscore[pl.ds(b, 1), :] = score.T[0:1, :]
        return 0

    lax.fori_loop(0, blocks, gold_block, 0)

    def step(j, _):
        for i, events in enumerate(EVENTS):
            if events:
                pl.when(j == i)(functools.partial(handle, events))
        slot = jnp.int32(ORDER[0])
        for i in range(1, len(ORDER)):
            slot = jnp.where(j == i, ORDER[i], slot)
        for p in range(PIECES + 1):
            twin_arrival(slot, p).wait_recv()
        block = jnp.concatenate([buf[slot, 0], buf[slot, 1]], axis=0)
        scores = lax.dot_general(
            men[...], block, (((1,), (1,)), ((), ())), preferred_element_type=jnp.float32
        )
        owner = gid[...]
        left = jnp.where(ids[slot, 0].astype(jnp.float32) == owner, NEG, scores[:, :128])
        right = jnp.where(ids[slot, 1].astype(jnp.float32) == owner, NEG, scores[:, 128:])
        top = jnp.max(jnp.maximum(left, right), axis=1, keepdims=True)
        before = run[...]
        newest = jnp.maximum(before, top)
        shrink = jnp.exp(before - newest)
        left = jnp.exp(left - newest)
        right = jnp.exp(right - newest)
        run[...] = newest
        low[...] = low[...] * shrink + (left + right)
        weights = jnp.concatenate([left.astype(jnp.bfloat16), right.astype(jnp.bfloat16)], axis=1)
        terms = jnp.dot(weights, block, preferred_element_type=jnp.float32)
        for f in range(0, terms.shape[1], 128):
            u[:, f:f + 128] = u[:, f:f + 128] * shrink + terms[:, f:f + 128]
        return 0

    lax.fori_loop(0, len(ORDER), step, 0)

    lane = lax.broadcasted_iota(jnp.int32, (128, 128), 1)

    def settle_block(b, _):
        s = pl.ds(pl.multiple_of(b * 128, 128), 128)
        size = jnp.maximum(jnp.max(jnp.abs(u[s, :]), axis=1, keepdims=True), TINY)
        total = jnp.sum(low[s, :], axis=1, keepdims=True)
        cols = jnp.where(lane == 0, run[s, :], jnp.where(lane == 1, total, size))
        turn = cols.T
        stat[pl.ds(b, 1), :] = turn[0:1, :]
        stat[pl.ds(blocks + b, 1), :] = turn[1:2, :]
        stat[pl.ds(2 * blocks + b, 1), :] = turn[2:3, :]
        q[s, :] = jnp.round(u[s, :] * (LEVELS / size)).astype(jnp.int32).astype(jnp.int16)
        return 0

    lax.fori_loop(0, blocks, settle_block, 0)

    def peer_row(dx, dy):
        return ((n // NX + dy) % 2) * NX + (x + dx) % NX

    stat_copies, q_copies = [], []
    for e, (dx, dy) in enumerate(PEERS):
        there = peer(dx, dy, 1)
        stat_copies.append(pltpu.make_async_remote_copy(
            src_ref=stat, dst_ref=rstat.at[e], send_sem=ss.at[e], recv_sem=sr.at[e],
            device_id=there, device_id_type=MESH))
        first = pl.multiple_of(peer_row(dx, dy) * part, part)
        q_copies.append(pltpu.make_async_remote_copy(
            src_ref=q.at[pl.ds(first, part)], dst_ref=rq.at[e], send_sem=qs.at[e], recv_sem=qr.at[e],
            device_id=there, device_id_type=MESH))
    for cp in stat_copies:
        cp.start()
    for cp in q_copies:
        cp.start()
    for cp in stat_copies:
        cp.wait_recv()

    golds = gscore[...]
    tops = [stat[0:blocks, :]] + [rstat[e, 0:blocks, :] for e in range(len(PEERS))]
    sums = [stat[blocks:2 * blocks, :]] + [rstat[e, blocks:2 * blocks, :] for e in range(len(PEERS))]
    highest = golds
    for t in tops:
        highest = jnp.maximum(highest, t)
    whole = jnp.exp(golds - highest)
    for t, s in zip(tops, sums):
        whole = whole + s * jnp.exp(t - highest)
    lse = highest + jnp.log(whole)
    loss_ref[...] = lse - golds
    gscore[...] = jnp.exp(golds - lse) - 1.0
    run[0:blocks, :] = lse

    mine = (n * part) // 128
    row = pl.ds(mine, 1)
    my_lse = run[row, :]
    fac[0:1, :] = jnp.exp(stat[row, :] - my_lse)
    fac[1:2, :] = gscore[row, :]
    for e in range(len(PEERS)):
        size = rstat[e, pl.ds(2 * blocks + mine, 1), :] * (1.0 / LEVELS)
        fac[2 + e:3 + e, :] = size * jnp.exp(rstat[e, row, :] - my_lse)
    turned[...] = fac[...].T
    f = turned[pl.ds(pl.multiple_of((n * part) % 128, part), part), :]
    own = pl.ds(pl.multiple_of(n * part, part), part)
    grad_ref[...] = u[own, :] * f[:, 0:1] + gold[own, :].astype(jnp.float32) * f[:, 1:2]
    for e in range(len(PEERS)):
        q_copies[e].wait_recv()
        grad_ref[...] += rq[e].astype(jnp.int32).astype(jnp.float32) * f[:, 2 + e:3 + e]

    for p in range(PIECES + 1):
        for k in range(1, 8):
            z_copy(k, k, up, p).wait_send()
        for k in range(8):
            y_copy(k, p).wait_send()
        for k in range(16):
            twin_copy(k, p).wait_send()
    for cp in stat_copies + q_copies:
        cp.wait_send()


def per_device(mentions, gold_vectors, gold_ids, cache, cache_ids):
    count, features = mentions.shape
    rows = cache.shape[0]
    blocks = count // 128
    part = count // 8
    near = len(PEERS)
    any_ = pl.BlockSpec(memory_space=pl.ANY)
    vmem = pl.BlockSpec(memory_space=pltpu.VMEM)
    dma = pltpu.SemaphoreType.DMA
    loss, grad = pl.pallas_call(
        kernel,
        out_shape=(
            jax.ShapeDtypeStruct((blocks, 128), jnp.float32),
            jax.ShapeDtypeStruct((part, features), jnp.float32),
        ),
        in_specs=[any_, any_, vmem, any_, vmem],
        out_specs=(vmem, vmem),
        scratch_shapes=[
            pltpu.VMEM((16, 2, rows, features), jnp.bfloat16),
            pltpu.VMEM((16, 2, 1, rows), jnp.int32),
            pltpu.VMEM((count, features), jnp.bfloat16),
            pltpu.VMEM((count, features), jnp.bfloat16),
            pltpu.VMEM((count, 128), jnp.float32),
            pltpu.VMEM((blocks, 128), jnp.float32),
            pltpu.VMEM((count, 128), jnp.float32),
            pltpu.VMEM((count, 128), jnp.float32),
            pltpu.VMEM((count, features), jnp.float32),
            pltpu.VMEM((count, features), jnp.int16),
            pltpu.VMEM((near, part, features), jnp.int16),
            pltpu.VMEM((4 * blocks, 128), jnp.float32),
            pltpu.VMEM((near, 4 * blocks, 128), jnp.float32),
            pltpu.VMEM((128, 128), jnp.float32),
            pltpu.VMEM((128, 128), jnp.float32),
            dma((3,)),
            dma((8, PIECES + 1)),
            dma((8, PIECES + 1)),
            dma((8, PIECES + 1)),
            dma((8, PIECES + 1)),
            dma((16, PIECES + 1)),
            dma((16, PIECES + 1)),
            dma((near,)),
            dma((near,)),
            dma((near,)),
            dma((near,)),
        ],
        compiler_params=pltpu.CompilerParams(
            collective_id=0, has_side_effects=True, vmem_limit_bytes=40 * 2**20
        ),
        name="linking",
    )(mentions, gold_vectors, gold_ids.reshape(blocks, 128), cache, cache_ids.reshape(1, rows))
    return loss.reshape(count), grad


def solution(mesh):
    in_specs = (
        P("wide", None),
        P("wide", None),
        P("wide"),
        P(("wide", "narrow"), None),
        P(("wide", "narrow")),
    )
    out_specs = (P("wide"), P(("wide", "narrow"), None))
    return jax.shard_map(
        per_device, mesh=mesh, in_specs=in_specs, out_specs=out_specs, check_vma=False
    )
```

```python
import functools

import jax
import jax.numpy as jnp
from jax import lax
from jax.experimental import pallas as pl
from jax.experimental.pallas import tpu as pltpu
from jax.sharding import PartitionSpec as P

MESH = pl.DeviceIdType.MESH
NEG = -1e30
FLOOR = -1e20
NX, NY, NZ = 4, 4, 8
LEVELS = 32766.0
TINY = 1e-35
PEERS = ((2, 1), (1, 1), (3, 1), (0, 1), (2, 0), (1, 0), (3, 0))
FAR = 4
GROUPS = ((0, 8), (1, 2), (3, 4), (9, 10), (5, 6), (11, 12), (7, 13), (14,), (15,))
ORDER = sum(GROUPS, ())
SLOT = {k: i for i, k in enumerate(ORDER)}
PAIRS = 7
PIECES = 2
IDS, WHOLE = PIECES, -1
EVENTS = (
    ((("y", 0),), (("z", 1), ("z", 2))),
    (),
    ((("z", 3), ("z", 4)), (("y", 1),)),
    ((("y", 2),), (("z", 5), ("z", 6))),
    ((("y", 3),),),
    ((("y", 4),), (("z", 7),)),
    ((("y", 5),),),
    ((("y", 6),),),
    ((("y", 7),),),
)


def place(x, y, z, c):
    return ((y % 2 * NZ + z) * 2 + c, (y // 2) * NX + x)


def kernel(
    mentions_hbm, gold_hbm, gold_ids_hbm, cache_hbm, cache_ids_hbm, loss_ref, grad_ref,
    buf, ids, gids, men, gold, gid, gscore, run, low, u, q, rq, stat, rstat, fac, turned,
    local_sem, zs, zr, ys, yr, cs, cr, qs, qr, ss, sr,
):
    w = lax.axis_index("wide")
    n = lax.axis_index("narrow")
    c = w % 2
    z = (w // 2) % NZ
    y = (n // NX) * 2 + w // (2 * NZ)
    x = n % NX
    rows = buf.shape[2]
    piece = rows // PIECES
    count = men.shape[0]
    blocks = count // 128
    half = count // 2
    part = grad_ref.shape[0]
    way = 1 - 2 * c

    ahead = place(x, y, (z + NZ + way) % NZ, c)
    behind = place(x, y, (z + NZ - way) % NZ, c)
    side = place(x, (y + NY + way) % NY, z, c)
    other_side = place(x, (y + NY - way) % NY, z, c)
    twin = place(x, y, z, 1 - c)

    def peer(dx, dy, sign):
        return place((x + NX + sign * dx) % NX, (y + 2 * dy) % NY, z, c)

    load_c = pltpu.make_async_copy(cache_hbm, buf.at[SLOT[0], c], local_sem.at[0])
    load_i = pltpu.make_async_copy(cache_ids_hbm, ids.at[SLOT[0], c], local_sem.at[1])
    load_n = pltpu.make_async_copy(gold_ids_hbm, gids, local_sem.at[2])
    load_m = pltpu.make_async_copy(mentions_hbm, men, local_sem.at[3])
    load_g = pltpu.make_async_copy(gold_hbm, gold, local_sem.at[4])
    for cp in (load_c, load_i, load_n, load_m, load_g):
        cp.start()

    barrier = pltpu.get_barrier_semaphore()
    sources = [ahead, behind, other_side, twin] + [peer(dx, dy, -1) for dx, dy in PEERS]
    for d in sources:
        pl.semaphore_signal(barrier, inc=1, device_id=d, device_id_type=MESH)

    def moved(what, src, dst, send, recv, index, core, target, own=False):
        if what == IDS:
            source, goal = ids.at[src, core], ids.at[dst, core]
        elif what == WHOLE:
            source, goal = buf.at[src, core], buf.at[dst, core]
        else:
            s = pl.ds(what * piece, piece)
            source, goal = buf.at[src, core, s], buf.at[dst, core, s]
        i = 0 if what == WHOLE else what
        if own:
            source = cache_ids_hbm if what == IDS else cache_hbm
            source = source.at[s] if 0 <= what < PIECES else source
        return pltpu.make_async_remote_copy(
            src_ref=source, dst_ref=goal, send_sem=send.at[index, i], recv_sem=recv.at[index, i],
            device_id=target, device_id_type=MESH)

    def z_copy(what, src, dst, target):
        return moved(what, SLOT[src], SLOT[dst], zs, zr, dst, c, target, own=src == 0)

    def y_copy(what, k):
        return moved(what, SLOT[k], SLOT[8 + k], ys, yr, k, c, side, own=k == 0)

    def twin_copy(what, slot):
        return moved(what, slot, slot, cs, cr, slot, c, twin, own=slot == SLOT[0])

    def twin_arrival(what, slot):
        return moved(what, slot, slot, cs, cr, slot, 1 - c, twin)

    def to_twin(what, slot):
        if what == IDS:
            twin_copy(IDS, slot).start()
        elif what == PIECES - 1:
            twin_copy(WHOLE, slot).start()

    def handle(events):
        for together in events:
            for what in (IDS,) + tuple(range(PIECES)):
                for kind, k in together:
                    if kind == "z":
                        z_copy(what, k, k, ahead).wait_recv()
                        if k <= 5:
                            z_copy(what, k, k + 2, ahead if k % 2 else behind).start()
                        y_copy(what, k).start()
                        to_twin(what, SLOT[k])
                    else:
                        y_copy(what, k).wait_recv()
                        to_twin(what, SLOT[8 + k])

    pl.semaphore_wait(barrier, len(sources))
    for what in (IDS,) + tuple(range(PIECES)):
        z_copy(what, 0, 1, ahead).start()
        z_copy(what, 0, 2, behind).start()
        y_copy(what, 0).start()
        to_twin(what, SLOT[0])

    run[...] = jnp.full(run.shape, FLOOR, jnp.float32)
    low[...] = jnp.zeros(low.shape, jnp.float32)
    u[...] = jnp.zeros(u.shape, jnp.float32)
    fac[...] = jnp.zeros(fac.shape, jnp.float32)
    load_n.wait()
    load_i.wait()
    load_c.wait()
    for b in range(blocks):
        row = jnp.broadcast_to(gids[pl.ds(b, 1), :].astype(jnp.float32), (128, 128))
        gid[pl.ds(b * 128, 128), :] = row.T

    load_m.wait()
    load_g.wait()

    def gold_block(b, _):
        s = pl.ds(pl.multiple_of(b * 128, 128), 128)
        both = men[s, :].astype(jnp.float32) * gold[s, :].astype(jnp.float32)
        score = jnp.broadcast_to(jnp.sum(both, axis=1, keepdims=True), (128, 128))
        gscore[pl.ds(b, 1), :] = score.T[0:1, :]
        return 0

    lax.fori_loop(0, blocks, gold_block, 0)

    def attend(slot, width, first):
        s = pl.ds(first, half)
        block = buf[pl.ds(slot, width)].reshape(2 * width * rows, buf.shape[3])
        scores = lax.dot_general(
            men[s, :], block, (((1,), (1,)), ((), ())), preferred_element_type=jnp.float32
        )
        owner = gid[s, :]
        parts = []
        for i in range(2 * width):
            named = ids[slot + i // 2, i % 2].astype(jnp.float32)
            parts.append(jnp.where(named == owner, NEG, scores[:, rows * i:rows * (i + 1)]))
        before = run[s, :]
        newest = jnp.maximum(before, jnp.max(functools.reduce(jnp.maximum, parts), axis=1, keepdims=True))
        shrink = jnp.exp(before - newest)
        parts = [jnp.exp(t - newest) for t in parts]
        run[s, :] = newest
        low[s, :] = low[s, :] * shrink + functools.reduce(jnp.add, parts)
        weights = jnp.concatenate([t.astype(jnp.bfloat16) for t in parts], axis=1)
        terms = jnp.dot(weights, block, preferred_element_type=jnp.float32)
        for f in range(0, terms.shape[1], 128):
            u[s, f:f + 128] = u[s, f:f + 128] * shrink + terms[:, f:f + 128]

    def twins(slot, width):
        for i in range(width):
            for what in (IDS, WHOLE):
                twin_arrival(what, slot + i).wait_recv()

    def step(j, _):
        for i, events in enumerate(EVENTS[:PAIRS]):
            if events:
                pl.when(j == i)(functools.partial(handle, events))
        twins(2 * j, 2)
        for h in range(2):
            attend(2 * j, 2, h * half)
        return 0

    lax.fori_loop(0, PAIRS, step, 0)

    lane = lax.broadcasted_iota(jnp.int32, (128, 128), 1)

    def settle(first):
        for i in range(half // 128):
            at = pl.multiple_of(first + i * 128, 128)
            s = pl.ds(at, 128)
            b = at // 128
            size = jnp.maximum(jnp.max(jnp.abs(u[s, :]), axis=1, keepdims=True), TINY)
            total = jnp.sum(low[s, :], axis=1, keepdims=True)
            cols = jnp.where(lane == 0, run[s, :], jnp.where(lane == 1, total, size))
            turn = cols.T
            stat[pl.ds(b, 1), :] = turn[0:1, :]
            stat[pl.ds(blocks + b, 1), :] = turn[1:2, :]
            stat[pl.ds(2 * blocks + b, 1), :] = turn[2:3, :]
            q[s, :] = jnp.round(u[s, :] * (LEVELS / size)).astype(jnp.int32).astype(jnp.int16)

    stat_copies, q_copies = [], []
    for e, (dx, dy) in enumerate(PEERS):
        there = peer(dx, dy, 1)
        owner_row = ((n // NX + dy) % 2) * NX + (x + dx) % NX
        first = pl.multiple_of(owner_row * part, part)
        stat_copies.append(pltpu.make_async_remote_copy(
            src_ref=stat, dst_ref=rstat.at[e], send_sem=ss.at[e], recv_sem=sr.at[e],
            device_id=there, device_id_type=MESH))
        q_copies.append(pltpu.make_async_remote_copy(
            src_ref=q.at[pl.ds(first, part)], dst_ref=rq.at[e], send_sem=qs.at[e], recv_sem=qr.at[e],
            device_id=there, device_id_type=MESH))

    far_rows = pl.multiple_of((1 - n // NX) * half, half)
    near_rows = pl.multiple_of((n // NX) * half, half)
    for i in range(PAIRS, len(GROUPS)):
        slot, width = SLOT[GROUPS[i][0]], len(GROUPS[i])
        handle(EVENTS[i])
        twins(slot, width)
        attend(slot, width, far_rows)
        if i < len(GROUPS) - 1:
            attend(slot, width, near_rows)
    settle(far_rows)
    for cp in q_copies[:FAR]:
        cp.start()
    attend(SLOT[15], 1, near_rows)
    settle(near_rows)
    for cp in stat_copies:
        cp.start()
    for cp in q_copies[FAR:]:
        cp.start()
    for cp in stat_copies:
        cp.wait_recv()

    golds = gscore[...]
    tops = [stat[0:blocks, :]] + [rstat[e, 0:blocks, :] for e in range(len(PEERS))]
    sums = [stat[blocks:2 * blocks, :]] + [rstat[e, blocks:2 * blocks, :] for e in range(len(PEERS))]
    highest = golds
    for t in tops:
        highest = jnp.maximum(highest, t)
    whole = jnp.exp(golds - highest)
    for t, t_sum in zip(tops, sums):
        whole = whole + t_sum * jnp.exp(t - highest)
    lse = highest + jnp.log(whole)
    loss_ref[...] = lse - golds
    gscore[...] = jnp.exp(golds - lse) - 1.0
    run[0:blocks, :] = lse

    mine = (n * part) // 128
    row = pl.ds(mine, 1)
    my_lse = run[row, :]
    fac[0:1, :] = jnp.exp(stat[row, :] - my_lse)
    fac[1:2, :] = gscore[row, :]
    for e in range(len(PEERS)):
        size = rstat[e, pl.ds(2 * blocks + mine, 1), :] * (1.0 / LEVELS)
        fac[2 + e:3 + e, :] = size * jnp.exp(rstat[e, row, :] - my_lse)
    turned[...] = fac[...].T
    f = turned[pl.ds(pl.multiple_of((n * part) % 128, part), part), :]
    own = pl.ds(pl.multiple_of(n * part, part), part)
    grad_ref[...] = u[own, :] * f[:, 0:1] + gold[own, :].astype(jnp.float32) * f[:, 1:2]
    for what in (IDS,) + tuple(range(PIECES)):
        for k in range(1, 8):
            z_copy(what, k, k, ahead).wait_send()
        for k in range(8):
            y_copy(what, k).wait_send()
    for what in (IDS, WHOLE):
        for k in range(16):
            twin_copy(what, k).wait_send()
    for e in range(len(PEERS)):
        q_copies[e].wait_recv()
        grad_ref[...] += rq[e].astype(jnp.int32).astype(jnp.float32) * f[:, 2 + e:3 + e]

    for cp in stat_copies + q_copies:
        cp.wait_send()


def per_device(mentions, gold_vectors, gold_ids, cache, cache_ids):
    count, features = mentions.shape
    rows = cache.shape[0]
    blocks = count // 128
    part = count // 8
    near = len(PEERS)
    any_ = pl.BlockSpec(memory_space=pl.ANY)
    vmem = pl.BlockSpec(memory_space=pltpu.VMEM)
    dma = pltpu.SemaphoreType.DMA
    loss, grad = pl.pallas_call(
        kernel,
        out_shape=(
            jax.ShapeDtypeStruct((blocks, 128), jnp.float32),
            jax.ShapeDtypeStruct((part, features), jnp.float32),
        ),
        in_specs=[any_] * 5,
        out_specs=(vmem, vmem),
        scratch_shapes=[
            pltpu.VMEM((16, 2, rows, features), jnp.bfloat16),
            pltpu.VMEM((16, 2, 1, rows), jnp.int32),
            pltpu.VMEM((blocks, 128), jnp.int32),
            pltpu.VMEM((count, features), jnp.bfloat16),
            pltpu.VMEM((count, features), jnp.bfloat16),
            pltpu.VMEM((count, 128), jnp.float32),
            pltpu.VMEM((blocks, 128), jnp.float32),
            pltpu.VMEM((count, 128), jnp.float32),
            pltpu.VMEM((count, 128), jnp.float32),
            pltpu.VMEM((count, features), jnp.float32),
            pltpu.VMEM((count, features), jnp.int16),
            pltpu.VMEM((near, part, features), jnp.int16),
            pltpu.VMEM((4 * blocks, 128), jnp.float32),
            pltpu.VMEM((near, 4 * blocks, 128), jnp.float32),
            pltpu.VMEM((128, 128), jnp.float32),
            pltpu.VMEM((128, 128), jnp.float32),
            dma((5,)),
            dma((8, PIECES + 1)),
            dma((8, PIECES + 1)),
            dma((8, PIECES + 1)),
            dma((8, PIECES + 1)),
            dma((16, PIECES + 1)),
            dma((16, PIECES + 1)),
            dma((near,)),
            dma((near,)),
            dma((near,)),
            dma((near,)),
        ],
        compiler_params=pltpu.CompilerParams(
            collective_id=0, has_side_effects=True, vmem_limit_bytes=55000 * 1024
        ),
        name="linking",
    )(mentions, gold_vectors, gold_ids.reshape(blocks, 128), cache, cache_ids.reshape(1, rows))
    return loss.reshape(count), grad


def solution(mesh):
    in_specs = (
        P("wide", None),
        P("wide", None),
        P("wide"),
        P(("wide", "narrow"), None),
        P(("wide", "narrow")),
    )
    out_specs = (P("wide"), P(("wide", "narrow"), None))
    return jax.shard_map(
        per_device, mesh=mesh, in_specs=in_specs, out_specs=out_specs, check_vma=False
    )
```

```python
import functools

import jax
import jax.numpy as jnp
from jax import lax
from jax.experimental import pallas as pl
from jax.experimental.pallas import tpu as pltpu
from jax.sharding import PartitionSpec as P

MESH = pl.DeviceIdType.MESH
NEG = -1e30
FLOOR = -1e20
NX, NY, NZ = 4, 4, 8
LEVELS = 32766.0
TINY = 1e-35
PEERS = ((2, 1), (1, 1), (3, 1), (0, 1), (2, 0), (1, 0), (3, 0))
FAR = 4
GROUPS = ((0, 8), (1, 2), (3, 4), (9, 10), (5, 6), (11, 12), (7, 13), (14,), (15,))
ORDER = sum(GROUPS, ())
SLOT = {k: i for i, k in enumerate(ORDER)}
PAIRS = 7
PIECES = 2
IDS, WHOLE = PIECES, -1
EVENTS = (
    ((("y", 0),), (("z", 1), ("z", 2))),
    (),
    ((("z", 3), ("z", 4)), (("y", 1),)),
    ((("y", 2),), (("z", 5), ("z", 6))),
    ((("y", 3),), (("y", 4),)),
    ((("z", 7),),),
    ((("y", 5),), (("y", 6),), (("y", 7),)),
    (),
    (),
)


def place(x, y, z, c):
    return ((y % 2 * NZ + z) * 2 + c, (y // 2) * NX + x)


def kernel(
    mentions_hbm, gold_hbm, gold_ids_hbm, cache_hbm, cache_ids_hbm, loss_ref, grad_ref,
    buf, ids, gids, men, gold, gid, gscore, run, low, u, q, rq, stat, rstat, fac, turned,
    local_sem, zs, zr, ys, yr, cs, cr, qs, qr, ss, sr,
):
    w = lax.axis_index("wide")
    n = lax.axis_index("narrow")
    c = w % 2
    z = (w // 2) % NZ
    y = (n // NX) * 2 + w // (2 * NZ)
    x = n % NX
    rows = buf.shape[2]
    piece = rows // PIECES
    count = men.shape[0]
    blocks = count // 128
    half = count // 2
    part = grad_ref.shape[0]
    way = 1 - 2 * c

    ahead = place(x, y, (z + NZ + way) % NZ, c)
    behind = place(x, y, (z + NZ - way) % NZ, c)
    side = place(x, (y + NY + way) % NY, z, c)
    other_side = place(x, (y + NY - way) % NY, z, c)
    twin = place(x, y, z, 1 - c)

    def peer(dx, dy, sign):
        return place((x + NX + sign * dx) % NX, (y + 2 * dy) % NY, z, c)

    load_c = pltpu.make_async_copy(cache_hbm, buf.at[SLOT[0], c], local_sem.at[0])
    load_i = pltpu.make_async_copy(cache_ids_hbm, ids.at[SLOT[0], c], local_sem.at[1])
    load_n = pltpu.make_async_copy(gold_ids_hbm, gids, local_sem.at[2])
    load_m = pltpu.make_async_copy(mentions_hbm, men, local_sem.at[3])
    load_g = pltpu.make_async_copy(gold_hbm, gold, local_sem.at[4])
    for cp in (load_c, load_i, load_n, load_m, load_g):
        cp.start()

    barrier = pltpu.get_barrier_semaphore()
    sources = [ahead, behind, other_side, twin] + [peer(dx, dy, -1) for dx, dy in PEERS]
    for d in sources:
        pl.semaphore_signal(barrier, inc=1, device_id=d, device_id_type=MESH)

    def moved(what, src, dst, send, recv, index, core, target, own=False):
        if what == IDS:
            source, goal = ids.at[src, core], ids.at[dst, core]
        elif what == WHOLE:
            source, goal = buf.at[src, core], buf.at[dst, core]
        else:
            s = pl.ds(what * piece, piece)
            source, goal = buf.at[src, core, s], buf.at[dst, core, s]
        i = 0 if what == WHOLE else what
        if own:
            source = cache_ids_hbm if what == IDS else cache_hbm
            source = source.at[s] if 0 <= what < PIECES else source
        return pltpu.make_async_remote_copy(
            src_ref=source, dst_ref=goal, send_sem=send.at[index, i], recv_sem=recv.at[index, i],
            device_id=target, device_id_type=MESH)

    def z_copy(what, src, dst, target):
        return moved(what, SLOT[src], SLOT[dst], zs, zr, dst, c, target, own=src == 0)

    def y_copy(what, k):
        return moved(what, SLOT[k], SLOT[8 + k], ys, yr, k, c, side, own=k == 0)

    def twin_copy(what, slot):
        return moved(what, slot, slot, cs, cr, slot, c, twin, own=slot == SLOT[0])

    def twin_arrival(what, slot):
        return moved(what, slot, slot, cs, cr, slot, 1 - c, twin)

    def to_twin(what, slot):
        if what == IDS:
            twin_copy(IDS, slot).start()
        else:
            twin_copy(what, slot).start()

    def handle(events):
        for together in events:
            for what in (IDS,) + tuple(range(PIECES)):
                for kind, k in together:
                    if kind == "z":
                        z_copy(what, k, k, ahead).wait_recv()
                        if k <= 5:
                            z_copy(what, k, k + 2, ahead if k % 2 else behind).start()
                        y_copy(what, k).start()
                        to_twin(what, SLOT[k])
                    else:
                        y_copy(what, k).wait_recv()
                        to_twin(what, SLOT[8 + k])

    pl.semaphore_wait(barrier, len(sources))
    for what in (IDS,) + tuple(range(PIECES)):
        z_copy(what, 0, 1, ahead).start()
        z_copy(what, 0, 2, behind).start()
        y_copy(what, 0).start()
        to_twin(what, SLOT[0])

    run[...] = jnp.full(run.shape, FLOOR, jnp.float32)
    low[...] = jnp.zeros(low.shape, jnp.float32)
    u[...] = jnp.zeros(u.shape, jnp.float32)
    fac[...] = jnp.zeros(fac.shape, jnp.float32)
    load_n.wait()
    load_i.wait()
    load_c.wait()
    for b in range(blocks):
        row = jnp.broadcast_to(gids[pl.ds(b, 1), :].astype(jnp.float32), (128, 128))
        gid[pl.ds(b * 128, 128), :] = row.T

    load_m.wait()
    load_g.wait()

    def gold_block(b, _):
        s = pl.ds(pl.multiple_of(b * 128, 128), 128)
        both = men[s, :].astype(jnp.float32) * gold[s, :].astype(jnp.float32)
        score = jnp.broadcast_to(jnp.sum(both, axis=1, keepdims=True), (128, 128))
        gscore[pl.ds(b, 1), :] = score.T[0:1, :]
        return 0

    lax.fori_loop(0, blocks, gold_block, 0)

    def attend(slot, width, first):
        s = pl.ds(first, half)
        block = buf[pl.ds(slot, width)].reshape(2 * width * rows, buf.shape[3])
        scores = lax.dot_general(
            men[s, :], block, (((1,), (1,)), ((), ())), preferred_element_type=jnp.float32
        )
        owner = gid[s, :]
        parts = []
        for i in range(2 * width):
            named = ids[slot + i // 2, i % 2].astype(jnp.float32)
            parts.append(jnp.where(named == owner, NEG, scores[:, rows * i:rows * (i + 1)]))
        before = run[s, :]
        newest = jnp.maximum(before, jnp.max(functools.reduce(jnp.maximum, parts), axis=1, keepdims=True))
        shrink = jnp.exp(before - newest)
        parts = [jnp.exp(t - newest) for t in parts]
        run[s, :] = newest
        low[s, :] = low[s, :] * shrink + functools.reduce(jnp.add, parts)
        weights = jnp.concatenate([t.astype(jnp.bfloat16) for t in parts], axis=1)
        terms = jnp.dot(weights, block, preferred_element_type=jnp.float32)
        for f in range(0, terms.shape[1], 128):
            u[s, f:f + 128] = u[s, f:f + 128] * shrink + terms[:, f:f + 128]

    def twins(slot, width):
        for i in range(width):
            for what in (IDS,) + tuple(range(PIECES)):
                twin_arrival(what, slot + i).wait_recv()

    def step(j, _):
        for i, events in enumerate(EVENTS[:PAIRS]):
            if events:
                pl.when(j == i)(functools.partial(handle, events))
        twins(2 * j, 2)
        for h in range(2):
            attend(2 * j, 2, h * half)
        return 0

    lax.fori_loop(0, PAIRS, step, 0)

    lane = lax.broadcasted_iota(jnp.int32, (128, 128), 1)

    def settle(first):
        sizes = []
        for i in range(half // 128):
            at = pl.multiple_of(first + i * 128, 128)
            s = pl.ds(at, 128)
            b = at // 128
            size = jnp.maximum(jnp.max(jnp.abs(u[s, :]), axis=1, keepdims=True), TINY)
            total = jnp.sum(low[s, :], axis=1, keepdims=True)
            cols = jnp.where(lane == 0, run[s, :], jnp.where(lane == 1, total, size))
            turn = cols.T
            stat[pl.ds(b, 1), :] = turn[0:1, :]
            stat[pl.ds(blocks + b, 1), :] = turn[1:2, :]
            stat[pl.ds(2 * blocks + b, 1), :] = turn[2:3, :]
            sizes.append((s, size))
        return sizes

    def quantize(sizes):
        for s, size in sizes:
            q[s, :] = jnp.round(u[s, :] * (LEVELS / size)).astype(jnp.int32).astype(jnp.int16)

    stat_copies, q_copies = [], []
    for e, (dx, dy) in enumerate(PEERS):
        there = peer(dx, dy, 1)
        owner_row = ((n // NX + dy) % 2) * NX + (x + dx) % NX
        first = pl.multiple_of(owner_row * part, part)
        stat_copies.append(pltpu.make_async_remote_copy(
            src_ref=stat, dst_ref=rstat.at[e], send_sem=ss.at[e], recv_sem=sr.at[e],
            device_id=there, device_id_type=MESH))
        q_copies.append(pltpu.make_async_remote_copy(
            src_ref=q.at[pl.ds(first, part)], dst_ref=rq.at[e], send_sem=qs.at[e], recv_sem=qr.at[e],
            device_id=there, device_id_type=MESH))

    far_rows = pl.multiple_of((1 - n // NX) * half, half)
    near_rows = pl.multiple_of((n // NX) * half, half)
    for i in range(PAIRS, len(GROUPS)):
        slot, width = SLOT[GROUPS[i][0]], len(GROUPS[i])
        handle(EVENTS[i])
        twins(slot, width)
        attend(slot, width, far_rows)
        if i < len(GROUPS) - 1:
            attend(slot, width, near_rows)
    quantize(settle(far_rows))
    for cp in q_copies[:FAR]:
        cp.start()
    attend(SLOT[15], 1, near_rows)
    sizes = settle(near_rows)
    for cp in stat_copies:
        cp.start()
    quantize(sizes)
    for cp in q_copies[FAR:]:
        cp.start()
    for cp in stat_copies:
        cp.wait_recv()

    golds = gscore[...]
    tops = [stat[0:blocks, :]] + [rstat[e, 0:blocks, :] for e in range(len(PEERS))]
    sums = [stat[blocks:2 * blocks, :]] + [rstat[e, blocks:2 * blocks, :] for e in range(len(PEERS))]
    highest = golds
    for t in tops:
        highest = jnp.maximum(highest, t)
    whole = jnp.exp(golds - highest)
    for t, t_sum in zip(tops, sums):
        whole = whole + t_sum * jnp.exp(t - highest)
    lse = highest + jnp.log(whole)
    loss_ref[...] = lse - golds
    gscore[...] = jnp.exp(golds - lse) - 1.0
    run[0:blocks, :] = lse

    mine = (n * part) // 128
    row = pl.ds(mine, 1)
    my_lse = run[row, :]
    fac[0:1, :] = jnp.exp(stat[row, :] - my_lse)
    fac[1:2, :] = gscore[row, :]
    for e in range(len(PEERS)):
        size = rstat[e, pl.ds(2 * blocks + mine, 1), :] * (1.0 / LEVELS)
        fac[2 + e:3 + e, :] = size * jnp.exp(rstat[e, row, :] - my_lse)
    turned[...] = fac[...].T
    f = turned[pl.ds(pl.multiple_of((n * part) % 128, part), part), :]
    own = pl.ds(pl.multiple_of(n * part, part), part)
    grad_ref[...] = u[own, :] * f[:, 0:1] + gold[own, :].astype(jnp.float32) * f[:, 1:2]
    for what in (IDS,) + tuple(range(PIECES)):
        for k in range(1, 8):
            z_copy(what, k, k, ahead).wait_send()
        for k in range(8):
            y_copy(what, k).wait_send()
    for what in (IDS,) + tuple(range(PIECES)):
        for k in range(16):
            twin_copy(what, k).wait_send()
    for e in range(len(PEERS)):
        q_copies[e].wait_recv()
        grad_ref[...] += rq[e].astype(jnp.int32).astype(jnp.float32) * f[:, 2 + e:3 + e]

    for cp in stat_copies + q_copies:
        cp.wait_send()


def per_device(mentions, gold_vectors, gold_ids, cache, cache_ids):
    count, features = mentions.shape
    rows = cache.shape[0]
    blocks = count // 128
    part = count // 8
    near = len(PEERS)
    any_ = pl.BlockSpec(memory_space=pl.ANY)
    vmem = pl.BlockSpec(memory_space=pltpu.VMEM)
    dma = pltpu.SemaphoreType.DMA
    loss, grad = pl.pallas_call(
        kernel,
        out_shape=(
            jax.ShapeDtypeStruct((blocks, 128), jnp.float32),
            jax.ShapeDtypeStruct((part, features), jnp.float32),
        ),
        in_specs=[any_] * 5,
        out_specs=(vmem, vmem),
        scratch_shapes=[
            pltpu.VMEM((16, 2, rows, features), jnp.bfloat16),
            pltpu.VMEM((16, 2, 1, rows), jnp.int32),
            pltpu.VMEM((blocks, 128), jnp.int32),
            pltpu.VMEM((count, features), jnp.bfloat16),
            pltpu.VMEM((count, features), jnp.bfloat16),
            pltpu.VMEM((count, 128), jnp.float32),
            pltpu.VMEM((blocks, 128), jnp.float32),
            pltpu.VMEM((count, 128), jnp.float32),
            pltpu.VMEM((count, 128), jnp.float32),
            pltpu.VMEM((count, features), jnp.float32),
            pltpu.VMEM((count, features), jnp.int16),
            pltpu.VMEM((near, part, features), jnp.int16),
            pltpu.VMEM((4 * blocks, 128), jnp.float32),
            pltpu.VMEM((near, 4 * blocks, 128), jnp.float32),
            pltpu.VMEM((128, 128), jnp.float32),
            pltpu.VMEM((128, 128), jnp.float32),
            dma((5,)),
            dma((8, PIECES + 1)),
            dma((8, PIECES + 1)),
            dma((8, PIECES + 1)),
            dma((8, PIECES + 1)),
            dma((16, PIECES + 1)),
            dma((16, PIECES + 1)),
            dma((near,)),
            dma((near,)),
            dma((near,)),
            dma((near,)),
        ],
        compiler_params=pltpu.CompilerParams(
            collective_id=0, has_side_effects=True, vmem_limit_bytes=55000 * 1024
        ),
        name="linking",
    )(mentions, gold_vectors, gold_ids.reshape(blocks, 128), cache, cache_ids.reshape(1, rows))
    return loss.reshape(count), grad


def solution(mesh):
    in_specs = (
        P("wide", None),
        P("wide", None),
        P("wide"),
        P(("wide", "narrow"), None),
        P(("wide", "narrow")),
    )
    out_specs = (P("wide"), P(("wide", "narrow"), None))
    return jax.shard_map(
        per_device, mesh=mesh, in_specs=in_specs, out_specs=out_specs, check_vma=False
    )
```

```python
import functools

import jax
import jax.numpy as jnp
from jax import lax
from jax.experimental import pallas as pl
from jax.experimental.pallas import tpu as pltpu
from jax.sharding import PartitionSpec as P

MESH = pl.DeviceIdType.MESH
NEG = -1e30
FLOOR = -1e20
NX, NY, NZ = 4, 4, 8
LEVELS = 32766.0
TINY = 1e-35
PEERS = ((2, 1), (1, 1), (3, 1), (0, 1), (2, 0), (1, 0), (3, 0))
FAR = 4
GROUPS = ((0, 8), (1, 2), (3, 4), (9, 10), (5, 6), (11, 12), (7, 13), (14,), (15,))
ORDER = sum(GROUPS, ())
SLOT = {k: i for i, k in enumerate(ORDER)}
PAIRS = 7
PIECES = 2
IDS, WHOLE = PIECES, -1
EVENTS = (
    ((("y", 0),), (("z", 1), ("z", 2))),
    (),
    ((("z", 3), ("z", 4)), (("y", 1),), (("y", 2),)),
    ((("z", 5), ("z", 6)),),
    ((("y", 3),), (("y", 4),)),
    ((("z", 7),),),
    ((("y", 5),), (("y", 6),), (("y", 7),)),
    (),
    (),
)


def place(x, y, z, c):
    return ((y % 2 * NZ + z) * 2 + c, (y // 2) * NX + x)


def kernel(
    mentions_hbm, gold_hbm, gold_ids_hbm, cache_hbm, cache_ids_hbm, loss_ref, grad_ref,
    buf, ids, gids, men, gold, gid, gscore, run, low, u, q, rq, stat, rstat, fac, turned,
    local_sem, zs, zr, ys, yr, cs, cr, qs, qr, ss, sr,
):
    w = lax.axis_index("wide")
    n = lax.axis_index("narrow")
    c = w % 2
    z = (w // 2) % NZ
    y = (n // NX) * 2 + w // (2 * NZ)
    x = n % NX
    rows = buf.shape[2]
    piece = rows // PIECES
    count = men.shape[0]
    blocks = count // 128
    half = count // 2
    part = grad_ref.shape[0]
    way = 1 - 2 * c

    ahead = place(x, y, (z + NZ + way) % NZ, c)
    behind = place(x, y, (z + NZ - way) % NZ, c)
    side = place(x, (y + NY + way) % NY, z, c)
    other_side = place(x, (y + NY - way) % NY, z, c)
    twin = place(x, y, z, 1 - c)

    def peer(dx, dy, sign):
        return place((x + NX + sign * dx) % NX, (y + 2 * dy) % NY, z, c)

    barrier = pltpu.get_barrier_semaphore()
    sources = [peer(dx, dy, -1) for dx, dy in PEERS] + [ahead, behind, other_side, twin]
    for d in sources:
        pl.semaphore_signal(barrier, inc=1, device_id=d, device_id_type=MESH)

    load_c = pltpu.make_async_copy(cache_hbm, buf.at[SLOT[0], c], local_sem.at[0])
    load_i = pltpu.make_async_copy(cache_ids_hbm, ids.at[SLOT[0], c], local_sem.at[1])
    load_n = pltpu.make_async_copy(gold_ids_hbm, gids, local_sem.at[2])
    load_m = pltpu.make_async_copy(mentions_hbm, men, local_sem.at[3])
    load_g = pltpu.make_async_copy(gold_hbm, gold, local_sem.at[4])
    for cp in (load_c, load_i, load_n, load_m, load_g):
        cp.start()

    def moved(what, src, dst, send, recv, index, core, target, own=False):
        if what == IDS:
            source, goal = ids.at[src, core], ids.at[dst, core]
        elif what == WHOLE:
            source, goal = buf.at[src, core], buf.at[dst, core]
        else:
            s = pl.ds(what * piece, piece)
            source, goal = buf.at[src, core, s], buf.at[dst, core, s]
        i = 0 if what == WHOLE else what
        if own:
            source = cache_ids_hbm if what == IDS else cache_hbm
            source = source.at[s] if 0 <= what < PIECES else source
        return pltpu.make_async_remote_copy(
            src_ref=source, dst_ref=goal, send_sem=send.at[index, i], recv_sem=recv.at[index, i],
            device_id=target, device_id_type=MESH)

    def z_copy(what, src, dst, target):
        return moved(what, SLOT[src], SLOT[dst], zs, zr, dst, c, target, own=src == 0)

    def y_copy(what, k):
        return moved(what, SLOT[k], SLOT[8 + k], ys, yr, k, c, side, own=k == 0)

    def twin_copy(what, slot):
        return moved(what, slot, slot, cs, cr, slot, c, twin, own=slot == SLOT[0])

    def twin_arrival(what, slot):
        return moved(what, slot, slot, cs, cr, slot, 1 - c, twin)

    def to_twin(what, slot):
        if what == IDS:
            twin_copy(IDS, slot).start()
        else:
            twin_copy(what, slot).start()

    def handle(events):
        for together in events:
            for what in (IDS,) + tuple(range(PIECES)):
                for kind, k in together:
                    if kind == "z":
                        z_copy(what, k, k, ahead).wait_recv()
                        if k <= 5:
                            z_copy(what, k, k + 2, ahead if k % 2 else behind).start()
                        y_copy(what, k).start()
                        to_twin(what, SLOT[k])
                    else:
                        y_copy(what, k).wait_recv()
                        to_twin(what, SLOT[8 + k])

    pl.semaphore_wait(barrier, len(sources))
    for what in (IDS,) + tuple(range(PIECES)):
        z_copy(what, 0, 1, ahead).start()
        z_copy(what, 0, 2, behind).start()
        y_copy(what, 0).start()
        to_twin(what, SLOT[0])

    run[...] = jnp.full(run.shape, FLOOR, jnp.float32)
    low[...] = jnp.zeros(low.shape, jnp.float32)
    u[...] = jnp.zeros(u.shape, jnp.float32)
    fac[...] = jnp.zeros(fac.shape, jnp.float32)
    load_n.wait()
    load_i.wait()
    load_c.wait()
    for b in range(blocks):
        row = jnp.broadcast_to(gids[pl.ds(b, 1), :].astype(jnp.float32), (128, 128))
        gid[pl.ds(b * 128, 128), :] = row.T

    load_m.wait()
    load_g.wait()

    def gold_block(b, _):
        s = pl.ds(pl.multiple_of(b * 128, 128), 128)
        both = men[s, :].astype(jnp.float32) * gold[s, :].astype(jnp.float32)
        score = jnp.broadcast_to(jnp.sum(both, axis=1, keepdims=True), (128, 128))
        gscore[pl.ds(b, 1), :] = score.T[0:1, :]
        return 0

    lax.fori_loop(0, blocks, gold_block, 0)

    def attend(slot, width, first):
        s = pl.ds(first, half)
        block = buf[pl.ds(slot, width)].reshape(2 * width * rows, buf.shape[3])
        scores = lax.dot_general(
            men[s, :], block, (((1,), (1,)), ((), ())), preferred_element_type=jnp.float32
        )
        owner = gid[s, :]
        parts = []
        for i in range(2 * width):
            named = ids[slot + i // 2, i % 2].astype(jnp.float32)
            parts.append(jnp.where(named == owner, NEG, scores[:, rows * i:rows * (i + 1)]))
        before = run[s, :]
        newest = jnp.maximum(before, jnp.max(functools.reduce(jnp.maximum, parts), axis=1, keepdims=True))
        shrink = jnp.exp(before - newest)
        parts = [jnp.exp(t - newest) for t in parts]
        run[s, :] = newest
        low[s, :] = low[s, :] * shrink + functools.reduce(jnp.add, parts)
        weights = jnp.concatenate([t.astype(jnp.bfloat16) for t in parts], axis=1)
        terms = jnp.dot(weights, block, preferred_element_type=jnp.float32)
        for f in range(0, terms.shape[1], 128):
            u[s, f:f + 128] = u[s, f:f + 128] * shrink + terms[:, f:f + 128]

    def twins(slot, width):
        for i in range(width):
            for what in (IDS,) + tuple(range(PIECES)):
                twin_arrival(what, slot + i).wait_recv()

    def step(j, _):
        for i, events in enumerate(EVENTS[:PAIRS]):
            if events:
                pl.when(j == i)(functools.partial(handle, events))
        twins(2 * j, 2)
        for h in range(2):
            attend(2 * j, 2, h * half)
        return 0

    lax.fori_loop(0, PAIRS, step, 0)

    lane = lax.broadcasted_iota(jnp.int32, (128, 128), 1)

    def settle(first):
        sizes = []
        for i in range(half // 128):
            at = pl.multiple_of(first + i * 128, 128)
            s = pl.ds(at, 128)
            b = at // 128
            size = jnp.maximum(jnp.max(jnp.abs(u[s, :]), axis=1, keepdims=True), TINY)
            total = jnp.sum(low[s, :], axis=1, keepdims=True)
            cols = jnp.where(lane == 0, run[s, :], jnp.where(lane == 1, total, size))
            turn = cols.T
            stat[pl.ds(b, 1), :] = turn[0:1, :]
            stat[pl.ds(blocks + b, 1), :] = turn[1:2, :]
            stat[pl.ds(2 * blocks + b, 1), :] = turn[2:3, :]
            sizes.append((s, size))
        return sizes

    def quantize(sizes):
        for s, size in sizes:
            q[s, :] = jnp.round(u[s, :] * (LEVELS / size)).astype(jnp.int32).astype(jnp.int16)

    stat_copies, q_copies = [], []
    for e, (dx, dy) in enumerate(PEERS):
        there = peer(dx, dy, 1)
        owner_row = ((n // NX + dy) % 2) * NX + (x + dx) % NX
        first = pl.multiple_of(owner_row * part, part)
        stat_copies.append(pltpu.make_async_remote_copy(
            src_ref=stat, dst_ref=rstat.at[e], send_sem=ss.at[e], recv_sem=sr.at[e],
            device_id=there, device_id_type=MESH))
        q_copies.append(pltpu.make_async_remote_copy(
            src_ref=q.at[pl.ds(first, part)], dst_ref=rq.at[e], send_sem=qs.at[e], recv_sem=qr.at[e],
            device_id=there, device_id_type=MESH))

    far_rows = pl.multiple_of((1 - n // NX) * half, half)
    near_rows = pl.multiple_of((n // NX) * half, half)
    for i in range(PAIRS, len(GROUPS)):
        slot, width = SLOT[GROUPS[i][0]], len(GROUPS[i])
        handle(EVENTS[i])
        twins(slot, width)
        attend(slot, width, far_rows)
        if i < len(GROUPS) - 1:
            attend(slot, width, near_rows)
    quantize(settle(far_rows))
    for cp in q_copies[:FAR]:
        cp.start()
    attend(SLOT[15], 1, near_rows)
    sizes = settle(near_rows)
    for cp in stat_copies:
        cp.start()
    quantize(sizes)
    for cp in q_copies[FAR:]:
        cp.start()
    for cp in stat_copies:
        cp.wait_recv()

    golds = gscore[...]
    tops = [stat[0:blocks, :]] + [rstat[e, 0:blocks, :] for e in range(len(PEERS))]
    sums = [stat[blocks:2 * blocks, :]] + [rstat[e, blocks:2 * blocks, :] for e in range(len(PEERS))]
    highest = golds
    for t in tops:
        highest = jnp.maximum(highest, t)
    whole = jnp.exp(golds - highest)
    for t, t_sum in zip(tops, sums):
        whole = whole + t_sum * jnp.exp(t - highest)
    lse = highest + jnp.log(whole)
    loss_ref[...] = lse - golds
    gscore[...] = jnp.exp(golds - lse) - 1.0
    run[0:blocks, :] = lse

    mine = (n * part) // 128
    row = pl.ds(mine, 1)
    my_lse = run[row, :]
    fac[0:1, :] = jnp.exp(stat[row, :] - my_lse)
    fac[1:2, :] = gscore[row, :]
    for e in range(len(PEERS)):
        size = rstat[e, pl.ds(2 * blocks + mine, 1), :] * (1.0 / LEVELS)
        fac[2 + e:3 + e, :] = size * jnp.exp(rstat[e, row, :] - my_lse)
    turned[...] = fac[...].T
    f = turned[pl.ds(pl.multiple_of((n * part) % 128, part), part), :]
    own = pl.ds(pl.multiple_of(n * part, part), part)
    grad_ref[...] = u[own, :] * f[:, 0:1] + gold[own, :].astype(jnp.float32) * f[:, 1:2]
    for what in (IDS,) + tuple(range(PIECES)):
        for k in range(1, 8):
            z_copy(what, k, k, ahead).wait_send()
        for k in range(8):
            y_copy(what, k).wait_send()
    for what in (IDS,) + tuple(range(PIECES)):
        for k in range(16):
            twin_copy(what, k).wait_send()
    for e in range(len(PEERS)):
        q_copies[e].wait_recv()
        grad_ref[...] += rq[e].astype(jnp.int32).astype(jnp.float32) * f[:, 2 + e:3 + e]

    for cp in stat_copies + q_copies:
        cp.wait_send()


def per_device(mentions, gold_vectors, gold_ids, cache, cache_ids):
    count, features = mentions.shape
    rows = cache.shape[0]
    blocks = count // 128
    part = count // 8
    near = len(PEERS)
    any_ = pl.BlockSpec(memory_space=pl.ANY)
    vmem = pl.BlockSpec(memory_space=pltpu.VMEM)
    dma = pltpu.SemaphoreType.DMA
    loss, grad = pl.pallas_call(
        kernel,
        out_shape=(
            jax.ShapeDtypeStruct((blocks, 128), jnp.float32),
            jax.ShapeDtypeStruct((part, features), jnp.float32),
        ),
        in_specs=[any_] * 5,
        out_specs=(vmem, vmem),
        scratch_shapes=[
            pltpu.VMEM((16, 2, rows, features), jnp.bfloat16),
            pltpu.VMEM((16, 2, 1, rows), jnp.int32),
            pltpu.VMEM((blocks, 128), jnp.int32),
            pltpu.VMEM((count, features), jnp.bfloat16),
            pltpu.VMEM((count, features), jnp.bfloat16),
            pltpu.VMEM((count, 128), jnp.float32),
            pltpu.VMEM((blocks, 128), jnp.float32),
            pltpu.VMEM((count, 128), jnp.float32),
            pltpu.VMEM((count, 128), jnp.float32),
            pltpu.VMEM((count, features), jnp.float32),
            pltpu.VMEM((count, features), jnp.int16),
            pltpu.VMEM((near, part, features), jnp.int16),
            pltpu.VMEM((4 * blocks, 128), jnp.float32),
            pltpu.VMEM((near, 4 * blocks, 128), jnp.float32),
            pltpu.VMEM((128, 128), jnp.float32),
            pltpu.VMEM((128, 128), jnp.float32),
            dma((5,)),
            dma((8, PIECES + 1)),
            dma((8, PIECES + 1)),
            dma((8, PIECES + 1)),
            dma((8, PIECES + 1)),
            dma((16, PIECES + 1)),
            dma((16, PIECES + 1)),
            dma((near,)),
            dma((near,)),
            dma((near,)),
            dma((near,)),
        ],
        compiler_params=pltpu.CompilerParams(
            collective_id=0, has_side_effects=True, vmem_limit_bytes=55000 * 1024
        ),
        name="linking",
    )(mentions, gold_vectors, gold_ids.reshape(blocks, 128), cache, cache_ids.reshape(1, rows))
    return loss.reshape(count), grad


def solution(mesh):
    in_specs = (
        P("wide", None),
        P("wide", None),
        P("wide"),
        P(("wide", "narrow"), None),
        P(("wide", "narrow")),
    )
    out_specs = (P("wide"), P(("wide", "narrow"), None))
    return jax.shard_map(
        per_device, mesh=mesh, in_specs=in_specs, out_specs=out_specs, check_vma=False
    )
```

```python
import functools

import jax
import jax.numpy as jnp
from jax import lax
from jax.experimental import pallas as pl
from jax.experimental.pallas import tpu as pltpu
from jax.sharding import PartitionSpec as P

MESH = pl.DeviceIdType.MESH
NEG = -1e30
FLOOR = -1e20
NX, NY, NZ = 4, 4, 8
LEVELS = 32766.0
TINY = 1e-30
PEERS = ((2, 1), (1, 1), (3, 1), (0, 1), (2, 0), (1, 0), (3, 0))
FAR = 4
GROUPS = ((0, 8), (1, 2), (3, 4), (9, 10), (5, 6), (11, 12), (7, 13), (14,), (15,))
ORDER = sum(GROUPS, ())
SLOT = {k: i for i, k in enumerate(ORDER)}
PAIRS = 7
PIECES = 2
IDS, WHOLE = PIECES, -1
EVENTS = (
    ((("y", 0),), (("z", 1), ("z", 2))),
    (),
    ((("z", 3), ("z", 4)), (("y", 1), ("y", 2))),
    ((("z", 5), ("z", 6)),),
    ((("y", 3), ("y", 4)),),
    ((("z", 7),),),
    ((("y", 5), ("y", 6)), (("y", 7),)),
    (),
    (),
)


def place(x, y, z, c):
    return ((y % 2 * NZ + z) * 2 + c, (y // 2) * NX + x)


def kernel(
    mentions_hbm, gold_hbm, gold_ids_hbm, cache_hbm, cache_ids_hbm, loss_ref, grad_ref,
    buf, ids, gids, men, gold, gid, gscore, run, low, u, q, rq, stat, rstat, fac, turned,
    local_sem, zs, zr, ys, yr, cs, cr, qs, qr, ss, sr,
):
    w = lax.axis_index("wide")
    n = lax.axis_index("narrow")
    c = w % 2
    z = (w // 2) % NZ
    y = (n // NX) * 2 + w // (2 * NZ)
    x = n % NX
    rows = buf.shape[2]
    piece = rows // PIECES
    count = men.shape[0]
    blocks = count // 128
    half = count // 2
    part = grad_ref.shape[0]
    way = 1 - 2 * c

    ahead = place(x, y, (z + NZ + way) % NZ, c)
    behind = place(x, y, (z + NZ - way) % NZ, c)
    side = place(x, (y + NY + way) % NY, z, c)
    other_side = place(x, (y + NY - way) % NY, z, c)
    twin = place(x, y, z, 1 - c)

    def peer(dx, dy, sign):
        return place((x + NX + sign * dx) % NX, (y + 2 * dy) % NY, z, c)

    barrier = pltpu.get_barrier_semaphore()
    sources = [peer(dx, dy, -1) for dx, dy in PEERS] + [ahead, behind, other_side, twin]
    for d in sources:
        pl.semaphore_signal(barrier, inc=1, device_id=d, device_id_type=MESH)

    load_c = pltpu.make_async_copy(cache_hbm, buf.at[SLOT[0], c], local_sem.at[0])
    load_i = pltpu.make_async_copy(cache_ids_hbm, ids.at[SLOT[0], c], local_sem.at[1])
    load_n = pltpu.make_async_copy(gold_ids_hbm, gids, local_sem.at[2])
    load_m = pltpu.make_async_copy(mentions_hbm, men, local_sem.at[3])
    load_g = pltpu.make_async_copy(gold_hbm, gold, local_sem.at[4])
    for cp in (load_c, load_i, load_n, load_m, load_g):
        cp.start()

    def moved(what, src, dst, send, recv, index, core, target, own=False):
        if what == IDS:
            source, goal = ids.at[src, core], ids.at[dst, core]
        elif what == WHOLE:
            source, goal = buf.at[src, core], buf.at[dst, core]
        else:
            s = pl.ds(what * piece, piece)
            source, goal = buf.at[src, core, s], buf.at[dst, core, s]
        i = 0 if what == WHOLE else what
        if own:
            source = cache_ids_hbm if what == IDS else cache_hbm
            source = source.at[s] if 0 <= what < PIECES else source
        return pltpu.make_async_remote_copy(
            src_ref=source, dst_ref=goal, send_sem=send.at[index, i], recv_sem=recv.at[index, i],
            device_id=target, device_id_type=MESH)

    def z_copy(what, src, dst, target):
        return moved(what, SLOT[src], SLOT[dst], zs, zr, dst, c, target, own=src == 0)

    def y_copy(what, k):
        return moved(what, SLOT[k], SLOT[8 + k], ys, yr, k, c, side, own=k == 0)

    def twin_copy(what, slot):
        return moved(what, slot, slot, cs, cr, slot, c, twin, own=slot == SLOT[0])

    def twin_arrival(what, slot):
        return moved(what, slot, slot, cs, cr, slot, 1 - c, twin)

    def to_twin(what, slot):
        if what == IDS:
            twin_copy(IDS, slot).start()
        else:
            twin_copy(what, slot).start()

    def handle(events):
        for together in events:
            for what in (IDS,) + tuple(range(PIECES)):
                for kind, k in together:
                    if kind == "z":
                        z_copy(what, k, k, ahead).wait_recv()
                        if k <= 5:
                            z_copy(what, k, k + 2, ahead if k % 2 else behind).start()
                        y_copy(what, k).start()
                        to_twin(what, SLOT[k])
                    else:
                        y_copy(what, k).wait_recv()
                        to_twin(what, SLOT[8 + k])

    pl.semaphore_wait(barrier, len(sources))
    for what in (IDS,) + tuple(range(PIECES)):
        z_copy(what, 0, 1, ahead).start()
        z_copy(what, 0, 2, behind).start()
        y_copy(what, 0).start()
        to_twin(what, SLOT[0])

    run[...] = jnp.full(run.shape, FLOOR, jnp.float32)
    low[...] = jnp.zeros(low.shape, jnp.float32)
    u[...] = jnp.zeros(u.shape, jnp.float32)
    fac[...] = jnp.zeros(fac.shape, jnp.float32)
    load_n.wait()
    load_i.wait()
    load_c.wait()
    for b in range(blocks):
        row = jnp.broadcast_to(gids[pl.ds(b, 1), :].astype(jnp.float32), (128, 128))
        gid[pl.ds(b * 128, 128), :] = row.T

    load_m.wait()
    load_g.wait()

    def gold_block(b, _):
        s = pl.ds(pl.multiple_of(b * 128, 128), 128)
        both = men[s, :].astype(jnp.float32) * gold[s, :].astype(jnp.float32)
        score = jnp.broadcast_to(jnp.sum(both, axis=1, keepdims=True), (128, 128))
        gscore[pl.ds(b, 1), :] = score.T[0:1, :]
        return 0

    lax.fori_loop(0, blocks, gold_block, 0)

    def attend(slot, width, first):
        s = pl.ds(first, half)
        block = buf[pl.ds(slot, width)].reshape(2 * width * rows, buf.shape[3])
        scores = lax.dot_general(
            men[s, :], block, (((1,), (1,)), ((), ())), preferred_element_type=jnp.float32
        )
        owner = gid[s, :]
        parts = []
        for i in range(2 * width):
            named = ids[slot + i // 2, i % 2].astype(jnp.float32)
            parts.append(jnp.where(named == owner, NEG, scores[:, rows * i:rows * (i + 1)]))
        before = run[s, :]
        newest = jnp.maximum(before, jnp.max(functools.reduce(jnp.maximum, parts), axis=1, keepdims=True))
        shrink = jnp.exp(before - newest)
        parts = [jnp.exp(t - newest) for t in parts]
        run[s, :] = newest
        low[s, :] = low[s, :] * shrink + functools.reduce(jnp.add, parts)
        weights = jnp.concatenate([t.astype(jnp.bfloat16) for t in parts], axis=1)
        terms = jnp.dot(weights, block, preferred_element_type=jnp.float32)
        for f in range(0, terms.shape[1], 128):
            u[s, f:f + 128] = u[s, f:f + 128] * shrink + terms[:, f:f + 128]

    def twins(slot, width):
        for i in range(width):
            for what in (IDS,) + tuple(range(PIECES)):
                twin_arrival(what, slot + i).wait_recv()

    def step(j, _):
        for i, events in enumerate(EVENTS[:PAIRS]):
            if events:
                pl.when(j == i)(functools.partial(handle, events))
        twins(2 * j, 2)
        for h in range(2):
            attend(2 * j, 2, h * half)
        return 0

    lax.fori_loop(0, PAIRS, step, 0)

    lane = lax.broadcasted_iota(jnp.int32, (128, 128), 1)

    def settle(first):
        sizes = []
        for i in range(half // 128):
            at = pl.multiple_of(first + i * 128, 128)
            s = pl.ds(at, 128)
            b = at // 128
            size = jnp.maximum(jnp.max(jnp.abs(u[s, :]), axis=1, keepdims=True), TINY)
            total = jnp.sum(low[s, :], axis=1, keepdims=True)
            cols = jnp.where(lane == 0, run[s, :], jnp.where(lane == 1, total, size))
            turn = cols.T
            stat[pl.ds(b, 1), :] = turn[0:1, :]
            stat[pl.ds(blocks + b, 1), :] = turn[1:2, :]
            stat[pl.ds(2 * blocks + b, 1), :] = turn[2:3, :]
            sizes.append((s, size))
        return sizes

    def quantize(sizes):
        for s, size in sizes:
            q[s, :] = jnp.round(u[s, :] * (LEVELS / size)).astype(jnp.int32).astype(jnp.int16)

    stat_copies, q_copies = [], []
    for e, (dx, dy) in enumerate(PEERS):
        there = peer(dx, dy, 1)
        owner_row = ((n // NX + dy) % 2) * NX + (x + dx) % NX
        first = pl.multiple_of(owner_row * part, part)
        stat_copies.append(pltpu.make_async_remote_copy(
            src_ref=stat, dst_ref=rstat.at[e], send_sem=ss.at[e], recv_sem=sr.at[e],
            device_id=there, device_id_type=MESH))
        q_copies.append(pltpu.make_async_remote_copy(
            src_ref=q.at[pl.ds(first, part)], dst_ref=rq.at[e], send_sem=qs.at[e], recv_sem=qr.at[e],
            device_id=there, device_id_type=MESH))

    far_rows = pl.multiple_of((1 - n // NX) * half, half)
    near_rows = pl.multiple_of((n // NX) * half, half)
    for i in range(PAIRS, len(GROUPS)):
        slot, width = SLOT[GROUPS[i][0]], len(GROUPS[i])
        handle(EVENTS[i])
        twins(slot, width)
        attend(slot, width, far_rows)
        if i < len(GROUPS) - 1:
            attend(slot, width, near_rows)
    quantize(settle(far_rows))
    for cp in q_copies[:FAR]:
        cp.start()
    attend(SLOT[15], 1, near_rows)
    sizes = settle(near_rows)
    for cp in stat_copies:
        cp.start()
    quantize(sizes)
    for cp in q_copies[FAR:]:
        cp.start()
    for cp in stat_copies:
        cp.wait_recv()

    golds = gscore[...]
    tops = [stat[0:blocks, :]] + [rstat[e, 0:blocks, :] for e in range(len(PEERS))]
    sums = [stat[blocks:2 * blocks, :]] + [rstat[e, blocks:2 * blocks, :] for e in range(len(PEERS))]
    highest = golds
    for t in tops:
        highest = jnp.maximum(highest, t)
    whole = jnp.exp(golds - highest)
    for t, t_sum in zip(tops, sums):
        whole = whole + t_sum * jnp.exp(t - highest)
    lse = highest + jnp.log(whole)
    loss_ref[...] = lse - golds
    gscore[...] = jnp.exp(golds - lse) - 1.0
    run[0:blocks, :] = lse

    mine = (n * part) // 128
    row = pl.ds(mine, 1)
    my_lse = run[row, :]
    fac[0:1, :] = jnp.exp(stat[row, :] - my_lse)
    fac[1:2, :] = gscore[row, :]
    for e in range(len(PEERS)):
        size = rstat[e, pl.ds(2 * blocks + mine, 1), :] * (1.0 / LEVELS)
        fac[2 + e:3 + e, :] = size * jnp.exp(rstat[e, row, :] - my_lse)
    turned[...] = fac[...].T
    f = turned[pl.ds(pl.multiple_of((n * part) % 128, part), part), :]
    own = pl.ds(pl.multiple_of(n * part, part), part)
    grad_ref[...] = u[own, :] * f[:, 0:1] + gold[own, :].astype(jnp.float32) * f[:, 1:2]
    for what in (IDS,) + tuple(range(PIECES)):
        for k in range(1, 8):
            z_copy(what, k, k, ahead).wait_send()
        for k in range(8):
            y_copy(what, k).wait_send()
    for what in (IDS,) + tuple(range(PIECES)):
        for k in range(16):
            twin_copy(what, k).wait_send()
    for e in range(len(PEERS)):
        q_copies[e].wait_recv()
        grad_ref[...] += rq[e].astype(jnp.int32).astype(jnp.float32) * f[:, 2 + e:3 + e]

    for cp in stat_copies + q_copies:
        cp.wait_send()


def per_device(mentions, gold_vectors, gold_ids, cache, cache_ids):
    count, features = mentions.shape
    rows = cache.shape[0]
    blocks = count // 128
    part = count // 8
    near = len(PEERS)
    any_ = pl.BlockSpec(memory_space=pl.ANY)
    vmem = pl.BlockSpec(memory_space=pltpu.VMEM)
    dma = pltpu.SemaphoreType.DMA
    loss, grad = pl.pallas_call(
        kernel,
        out_shape=(
            jax.ShapeDtypeStruct((blocks, 128), jnp.float32),
            jax.ShapeDtypeStruct((part, features), jnp.float32),
        ),
        in_specs=[any_] * 5,
        out_specs=(vmem, vmem),
        scratch_shapes=[
            pltpu.VMEM((16, 2, rows, features), jnp.bfloat16),
            pltpu.VMEM((16, 2, 1, rows), jnp.int32),
            pltpu.VMEM((blocks, 128), jnp.int32),
            pltpu.VMEM((count, features), jnp.bfloat16),
            pltpu.VMEM((count, features), jnp.bfloat16),
            pltpu.VMEM((count, 128), jnp.float32),
            pltpu.VMEM((blocks, 128), jnp.float32),
            pltpu.VMEM((count, 128), jnp.float32),
            pltpu.VMEM((count, 128), jnp.float32),
            pltpu.VMEM((count, features), jnp.float32),
            pltpu.VMEM((count, features), jnp.int16),
            pltpu.VMEM((near, part, features), jnp.int16),
            pltpu.VMEM((4 * blocks, 128), jnp.float32),
            pltpu.VMEM((near, 4 * blocks, 128), jnp.float32),
            pltpu.VMEM((128, 128), jnp.float32),
            pltpu.VMEM((128, 128), jnp.float32),
            dma((5,)),
            dma((8, PIECES + 1)),
            dma((8, PIECES + 1)),
            dma((8, PIECES + 1)),
            dma((8, PIECES + 1)),
            dma((16, PIECES + 1)),
            dma((16, PIECES + 1)),
            dma((near,)),
            dma((near,)),
            dma((near,)),
            dma((near,)),
        ],
        compiler_params=pltpu.CompilerParams(
            collective_id=0, has_side_effects=True, vmem_limit_bytes=55000 * 1024
        ),
        name="linking",
    )(mentions, gold_vectors, gold_ids.reshape(blocks, 128), cache, cache_ids.reshape(1, rows))
    return loss.reshape(count), grad


def solution(mesh):
    in_specs = (
        P("wide", None),
        P("wide", None),
        P("wide"),
        P(("wide", "narrow"), None),
        P(("wide", "narrow")),
    )
    out_specs = (P("wide"), P(("wide", "narrow"), None))
    return jax.shard_map(
        per_device, mesh=mesh, in_specs=in_specs, out_specs=out_specs, check_vma=False
    )
```
